256 devices in a mesh: gx: 16 (over x, y), gy: 8 (over z), cores: 2 (over core).
Axes of the slice: x: 4, y: 4, z: 8, core: 2. Of those that a mesh axis runs over, the one named last changes fastest.
Arguments:
- conserved: float32 [5, 512, 512, 128], P(None, 'gx', ('gy', 'cores')), as said below
- box_level: int32 [32, 32], P('gx', ('gy', 'cores')), may hold values from 0 to 1
- box_owner: int32 [32, 32], P('gx', ('gy', 'cores')), may hold values from 0 to 15, as said below
Outputs:
- relocated: float32 [4096, 5, 16, 16, 128], P(('gx', 'gy', 'cores'))
The draws below stay inside these ranges and needn't reach their ends.
Inputs may be any that keep to these rules, and one draw needn't show every extreme that they name: `box_owner`: among the boxes of one device (an aligned 2 x 2 block of the box grid) no value occurs more than 1 times, and some value occurs exactly 1 times. `conserved`: density and pressure lie in 0.5 to 2 at every cell and each velocity component in -0.8 to 0.8.
All inputs are finite; a program needn't handle non-finite values.
Results may differ from the reference program's by a relative error of at most 0.0003.
Values sent between devices are 32-bit elements; how exact they have to be, the bound alone decides.
No kernel may reach another device: no remote copies, remote signals or barrier semaphores. Data moves between devices by JAX's collectives and lax.ppermute only.
A program may use at most 128 MiB of HBM per device.

```python
import math
import jax
import jax.numpy as jnp
from jax import lax

BS = 16
BZ = 128
BXD = 2
BYD = 2
CAP = 1
GBX = 32
GBY = 32
NX = 512
NY = 512
N_GX = 16
N_GY = 8
N_CORES = 2


def draw_conserved(key, part):
    key = jax.random.fold_in(key, 11)
    density_key, velocity_key, pressure_key = jax.random.split(key, 3)
    extent = (NX, NY, BZ)
    density = jnp.exp(jax.random.uniform(density_key, extent, jnp.float32, math.log(0.5), math.log(2.0)))
    velocity = jnp.clip(0.35 * jax.random.normal(velocity_key, (3,) + extent, jnp.float32), -0.8, 0.8)
    pressure = jnp.exp(jax.random.uniform(pressure_key, extent, jnp.float32, math.log(0.5), math.log(2.0)))
    energy = 2.5 * pressure + 0.5 * density * jnp.sum(velocity * velocity, axis=0)
    return jnp.stack([density, density * velocity[0], density * velocity[1], density * velocity[2], energy]).astype(jnp.float32)


def draw_box_owner(key, part):
    key = jax.random.fold_in(key, 23)
    peers = GBX // BXD
    tiles = GBY // BYD
    count = BXD * BYD

    def one_tile(tile_key):
        pair_key, rest_key, order_key = jax.random.split(tile_key, 3)
        paired = jax.random.randint(pair_key, (), 0, peers)
        others = jax.random.permutation(rest_key, (peers - 1) * CAP)[:count - CAP].astype(jnp.int32)
        others = others + CAP * (others // CAP >= paired).astype(jnp.int32)
        chosen = jnp.concatenate([paired * CAP + jnp.arange(CAP, dtype=jnp.int32), others])
        owners = chosen // CAP
        return owners[jax.random.permutation(order_key, count)]
    owners = jax.vmap(one_tile)(jax.random.split(key, peers * tiles))
    return owners.reshape((peers, tiles, BXD, BYD)).transpose((0, 2, 1, 3)).reshape((GBX, GBY)).astype(jnp.int32)


def set_ends(entries, own_key, smallest, largest):
    spot = [jax.random.randint(jax.random.fold_in(own_key, axis), (), 0, length) for axis, length in enumerate(entries.shape)]
    main_axis = entries.shape.index(max(entries.shape))
    neighbour = spot[:main_axis] + [(spot[main_axis] + 1) % entries.shape[main_axis]] + spot[main_axis + 1:]
    return entries.at[tuple(spot)].set(smallest).at[tuple(neighbour)].set(largest)


def setup_inputs(seed: int = 0) -> dict:
    arg_keys = jax.random.split(jax.random.key(seed), 4)
    return {
        "conserved": draw_conserved(jax.random.fold_in(arg_keys[3], 71), 0),
        "box_level": set_ends(jax.random.randint(arg_keys[1], (GBX, GBY), 0, 2), jax.random.fold_in(arg_keys[1], 1), 0, 1).astype(jnp.int32),
        "box_owner": draw_box_owner(jax.random.fold_in(arg_keys[3], 71), 0),
    }


heat_ratio = 1.4
step_ratio = 0.06

def physical_flux(cells, axis_dir):
    density = cells[0]
    velocity = cells[1 + axis_dir] / density
    kinetic = 0.5 * (cells[1] * cells[1] + cells[2] * cells[2] + cells[3] * cells[3]) / density
    pressure = (heat_ratio - 1.0) * (cells[4] - kinetic)
    sound_speed = jnp.sqrt(heat_ratio * pressure / density)
    momenta = [cells[1] * velocity, cells[2] * velocity, cells[3] * velocity]
    momenta[axis_dir] = momenta[axis_dir] + pressure
    flux = jnp.stack([cells[1 + axis_dir]] + momenta + [(cells[4] + pressure) * velocity])
    return (flux, jnp.abs(velocity) + sound_speed)

def rusanov_flux(lower, upper, axis_dir):
    flux_low, speed_low = physical_flux(lower, axis_dir)
    flux_up, speed_up = physical_flux(upper, axis_dir)
    return 0.5 * (flux_low + flux_up) - 0.5 * jnp.maximum(speed_low, speed_up) * (upper - lower)

def advance(field, ratio):
    inner = field[:, 1:-1, 1:-1]
    flux_x = rusanov_flux(field[:, :-1, 1:-1], field[:, 1:, 1:-1], 0)
    flux_y = rusanov_flux(field[:, 1:-1, :-1], field[:, 1:-1, 1:], 1)
    mirror = jnp.array([1.0, 1.0, 1.0, -1.0, 1.0], jnp.float32).reshape(5, 1, 1, 1)
    walled = jnp.concatenate([inner[..., :1] * mirror, inner, inner[..., -1:] * mirror], axis=3)
    flux_z = rusanov_flux(walled[..., :-1], walled[..., 1:], 2)
    change = flux_x[:, 1:] - flux_x[:, :-1] + (flux_y[:, :, 1:] - flux_y[:, :, :-1]) + (flux_z[..., 1:] - flux_z[..., :-1])
    return (inner - ratio * change, flux_x, flux_y)

def coarse_path(window):
    box_side = window.shape[1] - 4
    fresh, flux_x, flux_y = advance(window[:, 1:-1, 1:-1], step_ratio)
    return (fresh, step_ratio * flux_x[:, 0], step_ratio * flux_x[:, box_side], step_ratio * flux_y[:, :, 0], step_ratio * flux_y[:, :, box_side])

def fine_path(window):
    box_side = window.shape[1] - 4
    half_ratio = 0.5 * step_ratio
    middle, first_x, first_y = advance(window, half_ratio)
    fresh, second_x, second_y = advance(middle, half_ratio)
    return (fresh, half_ratio * (first_x[:, 1, 1:box_side + 1] + second_x[:, 0]), half_ratio * (first_x[:, box_side + 1, 1:box_side + 1] + second_x[:, box_side]), half_ratio * (first_y[:, 1:box_side + 1, 1] + second_y[:, :, 0]), half_ratio * (first_y[:, 1:box_side + 1, box_side + 1] + second_y[:, :, box_side]))

def both_paths(window, level_value):
    coarse_parts = coarse_path(window)
    fine_parts = fine_path(window)
    return tuple((jnp.where(level_value == 1, fine_part, coarse_part) for coarse_part, fine_part in zip(coarse_parts, fine_parts)))

def face_corrections(levels, lower_x, upper_x, lower_y, upper_y, after_x, before_x, after_y, before_y, level_ax, level_bx, level_ay, level_by):
    coarse = levels == 0.0

    def pick(flag, values):
        return jnp.where(flag[..., None, None, None], values, 0.0)
    return (pick(coarse & (level_bx == 1.0), before_x - lower_x), pick(coarse & (level_ax == 1.0), upper_x - after_x), pick(coarse & (level_by == 1.0), before_y - lower_y), pick(coarse & (level_ay == 1.0), upper_y - after_y))

def apply_corrections(fresh, terms):
    fresh = fresh.at[..., 0, :, :].add(terms[0])
    fresh = fresh.at[..., -1, :, :].add(terms[1])
    fresh = fresh.at[..., 0, :].add(terms[2])
    fresh = fresh.at[..., -1, :].add(terms[3])
    return fresh

def reference(conserved, box_level, box_owner):
    box_side = BS
    box_columns = BXD * N_GX
    box_rows = BYD * N_GY * N_CORES
    tiles = N_GY * N_CORES
    count = BXD * BYD
    padded = jnp.pad(conserved, ((0, 0), (2, 2), (2, 2), (0, 0)), mode='wrap')
    starts = (jnp.arange(box_rows) * box_side).astype(jnp.int32)

    def one_column(index):
        strip = lax.dynamic_slice_in_dim(padded, index * box_side, box_side + 4, 1)
        windows = jax.vmap(lambda begin: lax.dynamic_slice_in_dim(strip, begin, box_side + 4, 2))(starts)
        return jax.vmap(both_paths)(windows, box_level[index])
    fresh, lower_x, upper_x, lower_y, upper_y = lax.map(one_column, jnp.arange(box_columns, dtype=jnp.int32))
    levels = box_level.astype(jnp.float32)
    terms = face_corrections(levels, lower_x, upper_x, lower_y, upper_y, jnp.roll(lower_x, -1, 0), jnp.roll(upper_x, 1, 0), jnp.roll(lower_y, -1, 1), jnp.roll(upper_y, 1, 1), jnp.roll(levels, -1, 0), jnp.roll(levels, 1, 0), jnp.roll(levels, -1, 1), jnp.roll(levels, 1, 1))
    corrected = apply_corrections(fresh, terms)
    box_tiles = corrected.reshape((N_GX, BXD, tiles, BYD, 5, box_side, box_side, BZ))
    box_tiles = box_tiles.transpose((0, 2, 1, 3, 4, 5, 6, 7)).reshape((N_GX, tiles, count, 5, box_side, box_side, BZ))
    owner_tiles = box_owner.reshape((N_GX, BXD, tiles, BYD)).transpose((0, 2, 1, 3)).reshape((N_GX, tiles, count))

    def place_tile(boxes, owners):
        order = jnp.arange(count)
        earlier = (owners[:, None] == owners[None, :]) & (order[None, :] < order[:, None])
        slots = (owners * CAP + lax.optimization_barrier(jnp.sum(earlier, axis=1))).astype(jnp.int32)
        return jnp.zeros((N_GX * CAP,) + boxes.shape[1:], jnp.float32).at[slots].set(boxes)
    sent = jax.vmap(jax.vmap(place_tile))(box_tiles, owner_tiles)
    sent = sent.reshape((N_GX, tiles, N_GX, CAP, 5, box_side, box_side, BZ))
    sent = sent.transpose((2, 1, 0, 3, 4, 5, 6, 7))
    return sent.reshape((N_GX * tiles * N_GX * CAP, 5, box_side, box_side, BZ))
```

```python
import jax
import jax.numpy as jnp
from jax import lax
from jax.experimental import pallas as pl
from jax.experimental.pallas import tpu as pltpu
from jax.sharding import PartitionSpec as P

BS = 16
NB = 2
SIDE = BS * NB
DEPTH = 128
XE = SIDE + 4
GAMMA = 1.4
STEP = 0.06
HALF = 0.25 * STEP

TILES = 5
ROWS = 48


def prims(u):
    r, mx, my, mz, e = u
    inv = pl.reciprocal(r, approx=True)
    inv = inv * (2.0 - r * inv)
    vx, vy, vz = mx * inv, my * inv, mz * inv
    p = (GAMMA - 1.0) * (e - 0.5 * (mx * vx + my * vy + mz * vz))
    a = GAMMA * p * inv
    c = a * lax.rsqrt(a)
    return vx, vy, vz, p, c, e + p


def rusanov(ua, fa, sa, ub, fb, sb):
    s = jnp.maximum(sa, sb)
    return [(fa[c] + fb[c]) - s * (ub[c] - ua[c]) for c in range(5)]


def z_change(u, fz, sz, first, last):
    def up(v):
        return pltpu.roll(v, DEPTH - 1, 1)

    un = [up(v) for v in u]
    fn = [un[3]] + [up(v) for v in fz[1:]]
    face = rusanov(u, fz, sz, un, fn, up(sz))
    wall = 2.0 * fz[3]
    push = 2.0 * sz * u[3]
    change = []
    for c in range(5):
        if c == 3:
            f = jnp.where(last, wall + push, face[c])
            change.append(f - jnp.where(first, wall - push, pltpu.roll(f, 1, 1)))
        else:
            f = jnp.where(last, 0.0, face[c])
            change.append(f - pltpu.roll(f, 1, 1))
    return change


def kernel(
    level, owner, cons, xlo, xhi, ylo, yhi, send,
    w, mid, out, zero, fxp, yb, fb, fxw, fxm, fyw, ym, lvx, in_sem, lv_sem, zero_sem, out_sem,
):
    copies = [
        pltpu.make_async_copy(cons, w.at[:, pl.ds(2, SIDE), pl.ds(8, SIDE), :], in_sem.at[0]),
        pltpu.make_async_copy(xlo.at[pl.ds(0, 5)], w.at[:, pl.ds(0, 2), pl.ds(8, SIDE), :], in_sem.at[1]),
        pltpu.make_async_copy(xhi.at[pl.ds(0, 5)], w.at[:, pl.ds(SIDE + 2, 2), pl.ds(8, SIDE), :], in_sem.at[2]),
        pltpu.make_async_copy(xlo.at[5, 0], lvx.at[0], lv_sem.at[0]),
        pltpu.make_async_copy(xhi.at[5, 0], lvx.at[1], lv_sem.at[1]),
    ]
    for copy in copies:
        copy.start()

    own = [owner[i] for i in range(4)]
    zero[...] = jnp.zeros_like(zero)

    def filled(slot):
        return (own[0] == slot) | (own[1] == slot) | (own[2] == slot) | (own[3] == slot)

    for slot in range(16):
        @pl.when(jnp.logical_not(filled(slot)))
        def _():
            pltpu.make_async_copy(zero, send.at[slot], zero_sem.at[slot]).start()

    lev = [[level[NB * a + b].astype(jnp.float32) for b in range(NB)] for a in range(NB)]

    def stage(x, _):
        for c in range(5):
            hi = yhi[c, x]
            w[c, x, 0:2, :] = hi
            w[c, x, 40:42, :] = hi
            w[c, x, 6:8, :] = ylo[c, x]
        return 0

    lax.fori_loop(0, XE, stage, 0)

    line = jnp.ones((1, DEPTH), jnp.float32)
    for a in range(NB):
        below = ylo[5, 2 + BS * a, 0:1, :]
        above = yhi[5, 2 + BS * a, 0:1, :]
        coarse = [1.0 - lev[a][b] for b in range(NB)]
        ym[a, 0, 0:1, :] = line * (HALF * coarse[0] * lev[a][1])
        ym[a, 0, 1:2, :] = above * (HALF * coarse[1])
        ym[a, 1, 0:1, :] = below * (HALF * coarse[0])
        ym[a, 1, 1:2, :] = line * (HALF * coarse[1] * lev[a][0])

    for copy in copies:
        copy.wait()

    lane = lax.broadcasted_iota(jnp.int32, (8, DEPTH), 1)
    first, last = lane == 0, lane == DEPTH - 1

    def row(ref, x, t, shift=0):
        return [ref[c, x, 8 * t + shift : 8 * t + shift + 8, :] for c in range(5)]

    def x_side(u, q):
        vx, _, _, p, c, h = q
        return [u[1], u[1] * vx + p, u[2] * vx, u[3] * vx, h * vx], jnp.abs(vx) + c

    def keep_x(t, fx, sx):
        for c in range(4):
            fxp[c, 8 * t : 8 * t + 8, :] = fx[c + 1]
        fxp[4, 8 * t : 8 * t + 8, :] = sx

    def x_face(src, x, t, u, fx, sx):
        ua = row(src, x - 1, t)
        fa = [ua[1]] + [fxp[c, 8 * t : 8 * t + 8, :] for c in range(4)]
        return rusanov(ua, fa, fxp[4, 8 * t : 8 * t + 8, :], u, fx, sx)

    def keep_y(t, u, q):
        _, vy, _, p, c, h = q
        fy = [u[1] * vy, u[2] * vy + p, u[3] * vy, h * vy, jnp.abs(vy) + c]
        for c in range(5):
            yb[c, 8 * t : 8 * t + 8, :] = fy[c]
            if t == 0:
                yb[c, 40:48, :] = fy[c]

    def y_faces(src, x):
        for t in (4, 0, 1, 2, 3):
            ua, ub = row(src, x, t), row(src, x, t, 1)
            fa = [ua[2]] + [yb[c, 8 * t : 8 * t + 8, :] for c in range(4)]
            fn = [ub[2]] + [yb[c, 8 * t + 1 : 8 * t + 9, :] for c in range(4)]
            face = rusanov(ua, fa, yb[4, 8 * t : 8 * t + 8, :], ub, fn, yb[4, 8 * t + 1 : 8 * t + 9, :])
            for c in range(5):
                fb[c, 8 * t + 8 : 8 * t + 16, :] = face[c]
                if t == 4:
                    fb[c, 0:8, :] = face[c]

    def y_change(t):
        return [fb[c, 8 * t + 8 : 8 * t + 16, :] - fb[c, 8 * t + 7 : 8 * t + 15, :] for c in range(5)]

    def z_side(u, q):
        _, _, vz, p, c, h = q
        return [u[3], u[1] * vz, u[2] * vz, u[3] * vz + p, h * vz], jnp.abs(vz) + c

    def face_slot(x):
        back = x - 2
        return jnp.where(back % BS == 0, back // BS, 3)

    def start_row(src, x, tiles):
        for t in tiles:
            u = row(src, x, t)
            keep_x(t, *x_side(u, prims(u)))

    start_row(w, 0, range(TILES))

    def first_step(x, _):
        slot = face_slot(x)
        acc = []
        for t in range(TILES):
            u = row(w, x, t)
            q = prims(u)
            fx, sx = x_side(u, q)
            face = x_face(w, x, t, u, fx, sx)
            keep_x(t, fx, sx)
            keep_y(t, u, q)
            fz, sz = z_side(u, q)
            dz = z_change(u, fz, sz, first, last)
            for c in range(5):
                old = mid[c, x - 1, 8 * t : 8 * t + 8, :] - HALF * face[c]
                mid[c, x - 1, 8 * t : 8 * t + 8, :] = old
                if t == 0:
                    mid[c, x - 1, 40:48, :] = old
                else:
                    fxw[c, slot, 8 * t - 8 : 8 * t, :] = face[c]
            acc.append([(u[c], face[c] - dz[c]) for c in range(5)])
        y_faces(w, x)
        for t in range(TILES):
            dy = y_change(t)
            for c in range(5):
                value, change = acc[t][c]
                mid[c, x, 8 * t : 8 * t + 8, :] = value + HALF * (change - dy[c])
        for c in range(5):
            fyw[c, x, 0:3, :] = fb[c, pl.ds(15, 3, stride=16), :]
        return 0

    lax.fori_loop(1, XE, first_step, 0)

    start_row(mid, 1, range(1, TILES))

    def second_step(a):
        def body(x, _):
            slot = face_slot(x)
            acc = []
            for t in range(TILES):
                u = row(mid, x, t)
                q = prims(u)
                keep_y(t, u, q)
                if t == 0:
                    continue
                b = (t - 1) // 2
                fx, sx = x_side(u, q)
                face = x_face(mid, x, t, u, fx, sx)
                keep_x(t, fx, sx)
                fz, sz = z_side(u, q)
                dz = z_change(u, fz, sz, first, last)
                back = jnp.maximum(x - 3, 0)
                ab = jnp.where(x - 3 >= BS, lev[1][b], lev[0][b]) if a else lev[0][b]
                for c in range(5):
                    fxm[c, slot, 8 * t - 8 : 8 * t, :] = face[c]
                    here = out[c, back, 8 * t - 8 : 8 * t, :]
                    out[c, back, 8 * t - 8 : 8 * t, :] = here - (HALF * ab) * face[c]
                acc.append([(u[c], face[c] - dz[c]) for c in range(5)])
            y_faces(mid, x)
            for t in range(1, TILES):
                b = (t - 1) // 2
                fine = level[NB * a + b] == 1
                dy = y_change(t)
                for c in range(5):
                    value, change = acc[t - 1][c]
                    whole = 2.0 * value - w[c, x, 8 * t : 8 * t + 8, :]
                    half = value + HALF * (change - dy[c])
                    out[c, x - 2, 8 * t - 8 : 8 * t, :] = jnp.where(fine, half, whole)
            for c in range(5):
                low = fb[c, pl.ds(31, 2, stride=16), :] - fyw[c, x, 1:3, :]
                high = fb[c, pl.ds(15, 2, stride=16), :] - fyw[c, x, 0:2, :]
                out[c, x - 2, pl.ds(BS - 1, 2, stride=BS), :] -= ym[a, 0, 0:2, :] * low
                out[c, x - 2, pl.ds(0, 2, stride=BS), :] += ym[a, 1, 0:2, :] * high
            return 0

        return body

    lax.fori_loop(2, 2 + BS, second_step(0), 0)
    lax.fori_loop(2 + BS, 2 + SIDE, second_step(1), 0)
    for t in range(1, TILES):
        b = (t - 1) // 2
        u = row(mid, SIDE + 2, t)
        fx, sx = x_side(u, prims(u))
        face = x_face(mid, SIDE + 2, t, u, fx, sx)
        for c in range(5):
            fxm[c, 2, 8 * t - 8 : 8 * t, :] = face[c]
            out[c, SIDE - 1, 8 * t - 8 : 8 * t, :] -= (HALF * lev[1][b]) * face[c]

    for k in range(NB + 1):
        for t in range(1, TILES):
            b = (t - 1) // 2
            at = slice(8 * t - 8, 8 * t)
            below = lvx[0, at, :] if k == 0 else lev[k - 1][b]
            above = lvx[1, at, :] if k == NB else lev[k][b]
            for c in range(5):
                d = HALF * (fxm[c, k, at, :] - fxw[c, k, at, :])
                if k > 0:
                    out[c, BS * k - 1, at, :] -= ((1.0 - below) * above) * d
                if k < NB:
                    out[c, BS * k, at, :] += ((1.0 - above) * below) * d

    done = []
    for a in range(NB):
        for b in range(NB):
            i = NB * a + b
            copy = pltpu.make_async_copy(
                out.at[:, pl.ds(BS * a, BS), pl.ds(BS * b, BS), :], send.at[own[i]], out_sem.at[i]
            )
            copy.start()
            done.append(copy)
    for copy in done:
        copy.wait()
    for slot in range(16):
        @pl.when(jnp.logical_not(filled(slot)))
        def _():
            pltpu.make_async_copy(zero, send.at[slot], zero_sem.at[slot]).wait()


def update(level, owner, cons, xlo, xhi, ylo, yhi):
    def grid(rows):
        return pltpu.VMEM((5, rows, ROWS, DEPTH), jnp.float32)

    smem = pl.BlockSpec(memory_space=pltpu.SMEM)
    vmem = pl.BlockSpec(memory_space=pltpu.VMEM)
    hbm = pl.BlockSpec(memory_space=pl.ANY)
    return pl.pallas_call(
        kernel,
        out_shape=jax.ShapeDtypeStruct((16, 5, BS, BS, DEPTH), jnp.float32),
        in_specs=[smem, smem, hbm, hbm, hbm, vmem, vmem],
        out_specs=hbm,
        scratch_shapes=[
            grid(XE),
            grid(XE),
            pltpu.VMEM((5, SIDE, SIDE, DEPTH), jnp.float32),
            pltpu.VMEM((5, BS, BS, DEPTH), jnp.float32),
            pltpu.VMEM((5, 40, DEPTH), jnp.float32),
            pltpu.VMEM((5, ROWS, DEPTH), jnp.float32),
            pltpu.VMEM((5, ROWS, DEPTH), jnp.float32),
            pltpu.VMEM((5, 4, SIDE, DEPTH), jnp.float32),
            pltpu.VMEM((5, 4, SIDE, DEPTH), jnp.float32),
            pltpu.VMEM((5, XE, 8, DEPTH), jnp.float32),
            pltpu.VMEM((NB, 2, 8, DEPTH), jnp.float32),
            pltpu.VMEM((2, SIDE, DEPTH), jnp.float32),
            pltpu.SemaphoreType.DMA((3,)),
            pltpu.SemaphoreType.DMA((2,)),
            pltpu.SemaphoreType.DMA((16,)),
            pltpu.SemaphoreType.DMA((4,)),
        ],
        compiler_params=pltpu.CompilerParams(vmem_limit_bytes=40 * 1024 * 1024),
        cost_estimate=pl.CostEstimate(flops=50_000_000, bytes_accessed=14_000_000, transcendentals=600_000),
    )(level, owner, cons, xlo, xhi, ylo, yhi)


def shifted(block, axis, step):
    n = lax.axis_size(axis)
    return lax.ppermute(block, axis, [(i, (i + step) % n) for i in range(n)])


def body(conserved, box_level, box_owner):
    lev = box_level.astype(jnp.float32)
    rows = ("gy", "cores")

    def x_pack(cells, levels):
        plane = jnp.broadcast_to(jnp.repeat(levels, BS)[None, None, :, None], (1, 2, SIDE, DEPTH))
        return jnp.concatenate([cells, plane], axis=0)

    xlo = shifted(x_pack(conserved[:, SIDE - 2 :], lev[NB - 1]), "gx", 1)
    xhi = shifted(x_pack(conserved[:, :2], lev[0]), "gx", -1)

    def y_pack(at, levels):
        cells = jnp.concatenate([xlo[:5, :, at], conserved[:, :, at], xhi[:5, :, at]], axis=1)
        plane = jnp.pad(jnp.repeat(levels, BS), (2, 2))
        plane = jnp.broadcast_to(plane[None, :, None, None], (1, XE, 2, DEPTH))
        return jnp.concatenate([cells, plane], axis=0)

    ylo = shifted(y_pack(slice(SIDE - 2, SIDE), lev[:, NB - 1]), rows, 1)
    yhi = shifted(y_pack(slice(0, 2), lev[:, 0]), rows, -1)
    send = update(box_level.reshape(-1), box_owner.reshape(-1), conserved, xlo, xhi, ylo, yhi)
    return lax.all_to_all(send, "gx", split_axis=0, concat_axis=0, tiled=True)


def solution(mesh):
    rows = ("gy", "cores")
    return jax.shard_map(
        body,
        mesh=mesh,
        in_specs=(P(None, "gx", rows, None), P("gx", rows), P("gx", rows)),
        out_specs=P(("gx", "gy", "cores"), None, None, None, None),
        check_vma=False,
    )
```

```python
import jax
import jax.numpy as jnp
from jax import lax
from jax.experimental import pallas as pl
from jax.experimental.pallas import tpu as pltpu
from jax.sharding import PartitionSpec as P

BS = 16
NB = 2
SIDE = BS * NB
DEPTH = 128
XE = SIDE + 4
GAMMA = 1.4
STEP = 0.06
HALF = 0.25 * STEP

TILES = 4
HALO = 4
CHUNK = 8


def prims(u):
    r, mx, my, mz, e = u
    inv = pl.reciprocal(r, approx=True)
    inv = inv * (2.0 - r * inv)
    vx, vy, vz = mx * inv, my * inv, mz * inv
    p = (GAMMA - 1.0) * (e - 0.5 * (mx * vx + my * vy + mz * vz))
    a = GAMMA * p * inv
    c = a * lax.rsqrt(a)
    return vx, vy, vz, p, c, e + p


def x_side(u, q):
    vx, _, _, p, c, h = q
    return u, [u[1], u[1] * vx + p, u[2] * vx, u[3] * vx, h * vx], jnp.abs(vx) + c


def y_side(u, q):
    _, vy, _, p, c, h = q
    return u, [u[2], u[1] * vy, u[2] * vy + p, u[3] * vy, h * vy], jnp.abs(vy) + c


def z_side(u, q):
    _, _, vz, p, c, h = q
    return u, [u[3], u[1] * vz, u[2] * vz, u[3] * vz + p, h * vz], jnp.abs(vz) + c


def rusanov(lower, upper):
    ua, fa, sa = lower
    ub, fb, sb = upper
    s = jnp.maximum(sa, sb)
    return [(fa[c] + fb[c]) - s * (ub[c] - ua[c]) for c in range(5)]


def each(side, f, shared):
    u, fl, s = side
    nu = [f(v) for v in u]
    return nu, [nu[shared]] + [f(v) for v in fl[1:]], f(s)


def both(pred, a, b, shared):
    ua, fa, sa = a
    ub, fb, sb = b
    u = [jnp.where(pred, v, w) for v, w in zip(ua, ub)]
    f = [u[shared]] + [jnp.where(pred, v, w) for v, w in zip(fa[1:], fb[1:])]
    return u, f, jnp.where(pred, sa, sb)


def z_faces(side, first, last):
    u, fz, sz = side
    face = rusanov(side, each(side, lambda v: pltpu.roll(v, DEPTH - 1, 1), 3))
    wall = 2.0 * fz[3]
    push = 2.0 * sz * u[3]
    walls = jnp.where(first, wall - push, jnp.where(last, -wall - push, 0.0))
    return [jnp.where(last, 0.0, f) for f in face], walls


def kernel(
    level, owner, cons, xlo, xhi, ylo, yhi, send,
    wn, wg, md, out, zero, fxp, fzp, fxw, fxm, fyw, msk, lvx, in_sem, x_sem, zero_sem, out_sem,
):
    def part(x):
        return pltpu.make_async_copy(
            cons.at[:, pl.ds(x - 2, CHUNK)], wn.at[:, pl.ds(x, CHUNK)], in_sem.at[(x - 2) // CHUNK]
        )

    low = pltpu.make_async_copy(xlo.at[pl.ds(0, 5)], wn.at[:, pl.ds(0, 2)], x_sem.at[0])
    high = pltpu.make_async_copy(xhi.at[pl.ds(0, 5)], wn.at[:, pl.ds(SIDE + 2, 2)], x_sem.at[1])
    low_level = pltpu.make_async_copy(xlo.at[5, 0], lvx.at[0], x_sem.at[2])
    high_level = pltpu.make_async_copy(xhi.at[5, 0], lvx.at[1], x_sem.at[3])
    low.start()
    for i in range(SIDE // CHUNK):
        part(2 + CHUNK * i).start()
    for copy in (high, low_level, high_level):
        copy.start()

    own = [owner[i] for i in range(NB * NB)]
    lev = [[level[NB * a + b].astype(jnp.float32) for b in range(NB)] for a in range(NB)]

    def stage(x, _):
        for c in range(5):
            wg[c, x, 0:1, :] = ylo[c, x, 1:2, :]
            wg[c, x, 1:2, :] = ylo[c, x, 0:1, :]
            wg[c, x, 6:7, :] = yhi[c, x, 1:2, :]
            wg[c, x, 7:8, :] = yhi[c, x, 0:1, :]
        return 0

    lax.fori_loop(0, XE, stage, 0, unroll=2)

    zero[...] = jnp.zeros_like(zero)

    def filled(slot):
        return (own[0] == slot) | (own[1] == slot) | (own[2] == slot) | (own[3] == slot)

    for slot in range(16):
        @pl.when(jnp.logical_not(filled(slot)))
        def _():
            pltpu.make_async_copy(zero, send.at[slot], zero_sem.at[slot]).start()

    lane = lax.broadcasted_iota(jnp.int32, (8, DEPTH), 1)
    sub = lax.broadcasted_iota(jnp.int32, (8, DEPTH), 0)
    first, last = lane == 0, lane == DEPTH - 1
    bottom, top = sub == 0, sub == 7

    for a in range(NB):
        coarse = [1.0 - lev[a][b] for b in range(NB)]
        below = ylo[5, 2 + BS * a, 0:1, :]
        above = yhi[5, 2 + BS * a, 0:1, :]
        msk[a, 0, :, :] = jnp.where(sub < 4, lev[a][0], lev[a][1])
        msk[a, 1, :, :] = jnp.where(
            sub == 3, HALF * coarse[0] * lev[a][1], jnp.where(top, HALF * coarse[1] * above, 0.0)
        )
        msk[a, 2, :, :] = jnp.where(
            sub == 4, HALF * coarse[1] * lev[a][0], jnp.where(bottom, HALF * coarse[0] * below, 0.0)
        )

    def spread(ref, c, x, t):
        return ref[c, x, pl.ds(t, 8, stride=4), :]

    def load_w(x, t):
        if t == HALO:
            return [wg[c, x] for c in range(5)]
        return [spread(wn, c, x, t) for c in range(5)]

    def load_m(x, t):
        return [md[c, x, t] for c in range(5)]

    def keep_x(t, side):
        _, f, s = side
        for c in range(4):
            fxp[c, t] = f[c + 1]
        fxp[4, t] = s

    def x_face(load, x, t, side):
        u = load(x - 1, t)
        return rusanov((u, [u[1]] + [fxp[c, t] for c in range(4)], fxp[4, t]), side)

    def up(v):
        return pltpu.roll(v, 7, 0)

    def down(v):
        return pltpu.roll(v, 1, 0)

    def z_change(t):
        f = [fzp[c, t] for c in range(5)]
        return [v - pltpu.roll(v, 1, 1) for v in f]

    def sweep(load, x, whole):
        cells, faces, ends, change, side = [], [], [], [], []
        for t in range(TILES + 1):
            u = load(x, t)
            q = prims(u)
            side.append(y_side(u, q))
            if t < TILES or whole:
                sx = x_side(u, q)
                face = x_face(load, x, t, sx)
                keep_x(t, sx)
                dz = z_change(t)
                fz, walls = z_faces(z_side(u, q), first, last)
                for c in range(5):
                    fzp[c, t] = fz[c]
                cells.append(u)
                faces.append(face)
                ends.append([face[c] + dz[c] for c in range(5)])
                change.append([face[c] + walls if c == 3 else face[c] for c in range(5)])
            if 0 < t < TILES:
                fy = rusanov(side[t - 1], side[t])
                change[t - 1] = [change[t - 1][c] - fy[c] for c in range(5)]
                change[t] = [change[t][c] + fy[c] for c in range(5)]
        inner = rusanov(side[3], each(side[0], up, 2))
        edge = rusanov(both(top, side[3], side[4], 2), both(top, side[4], side[0], 2))
        after = [jnp.where(top, edge[c], inner[c]) for c in range(5)]
        before = [jnp.where(bottom, edge[c], down(inner[c])) for c in range(5)]
        change[3] = [change[3][c] - after[c] for c in range(5)]
        change[0] = [change[0][c] + before[c] for c in range(5)]
        if whole:
            outer = rusanov(both(top, side[4], each(side[4], up, 2), 2), both(top, each(side[4], down, 2), side[4], 2))
            for c in range(5):
                d = edge[c] - outer[c]
                change[4][c] = change[4][c] + jnp.where(top, d, -d)
        return cells, faces, ends, change, before, after

    def face_slot(x):
        back = x - 2
        return jnp.where(back % BS == 0, back // BS, 3)

    low.wait()
    for t in range(TILES + 1):
        u = load_w(0, t)
        keep_x(t, x_side(u, prims(u)))

    def first_step(x, _):
        @pl.when(((x - 2) % CHUNK == 0) & (x < SIDE + 2))
        def _():
            part(x).wait()

        @pl.when(x == SIDE + 2)
        def _():
            high.wait()

        slot = face_slot(x)
        cells, faces, ends, change, before, after = sweep(load_w, x, True)
        for c in range(5):
            for t in range(TILES + 1):
                md[c, x - 1, t] = md[c, x - 1, t] - HALF * ends[t][c]
                md[c, x, t] = cells[t][c] + HALF * change[t][c]
                if t < TILES:
                    fxw[c, slot, t] = faces[t][c]
            fyw[0, c, x] = before[c]
            fyw[1, c, x] = after[c]
        return 0

    lax.fori_loop(1, XE, first_step, 0)

    for t in range(TILES):
        u = load_m(1, t)
        keep_x(t, x_side(u, prims(u)))

    def second_step(x, _):
        slot = face_slot(x)
        row = jnp.maximum(x - 3, 0)
        fine_back = HALF * msk[row // BS, 0]
        a = (x - 2) // BS
        fine = msk[a, 0]
        coarse = 1.0 - fine
        fine_here = HALF * fine
        at_top, at_bottom = msk[a, 1], msk[a, 2]
        cells, faces, ends, change, before, after = sweep(load_m, x, False)
        for c in range(5):
            for t in range(TILES):
                fxm[c, slot, t] = faces[t][c]
                at = pl.ds(t, 8, stride=4)
                out[c, row, at, :] = out[c, row, at, :] - fine_back * ends[t][c]
                u = cells[t][c]
                v = u + coarse * (u - spread(wn, c, x, t)) + fine_here * change[t][c]
                if t == 0:
                    v = v + at_bottom * (before[c] - fyw[0, c, x])
                if t == 3:
                    v = v - at_top * (after[c] - fyw[1, c, x])
                out[c, x - 2, at, :] = v
        return 0

    def correct(k):
        below = lvx[0, pl.ds(0, 8, stride=4), :] if k == 0 else msk[k - 1, 0]
        above = lvx[1, pl.ds(0, 8, stride=4), :] if k == NB else msk[k, 0]
        to_below = (HALF * (1.0 - below)) * above
        to_above = (HALF * (1.0 - above)) * below
        for t in range(TILES):
            at = pl.ds(t, 8, stride=4)
            for c in range(5):
                d = fxm[c, k, t] - fxw[c, k, t]
                if k > 0:
                    out[c, BS * k - 1, at, :] = out[c, BS * k - 1, at, :] - to_below * d
                if k < NB:
                    out[c, BS * k, at, :] = out[c, BS * k, at, :] + to_above * d

    done = []

    def ship(a):
        for b in range(NB):
            i = NB * a + b
            copy = pltpu.make_async_copy(
                out.at[:, pl.ds(BS * a, BS), pl.ds(BS * b, BS), :], send.at[own[i]], out_sem.at[i]
            )
            copy.start()
            done.append(copy)

    lax.fori_loop(2, BS + 3, second_step, 0)
    low_level.wait()
    high_level.wait()
    correct(0)
    correct(1)
    ship(0)
    lax.fori_loop(BS + 3, SIDE + 2, second_step, 0)
    for t in range(TILES):
        u = load_m(SIDE + 2, t)
        face = x_face(load_m, SIDE + 2, t, x_side(u, prims(u)))
        dz = z_change(t)
        at = pl.ds(t, 8, stride=4)
        for c in range(5):
            fxm[c, 2, t] = face[c]
            out[c, SIDE - 1, at, :] = out[c, SIDE - 1, at, :] - (HALF * msk[NB - 1, 0]) * (face[c] + dz[c])
    correct(2)
    ship(1)
    for copy in done:
        copy.wait()
    for slot in range(16):
        @pl.when(jnp.logical_not(filled(slot)))
        def _():
            pltpu.make_async_copy(zero, send.at[slot], zero_sem.at[slot]).wait()


def update(level, owner, cons, xlo, xhi, ylo, yhi):
    smem = pl.BlockSpec(memory_space=pltpu.SMEM)
    vmem = pl.BlockSpec(memory_space=pltpu.VMEM)
    hbm = pl.BlockSpec(memory_space=pl.ANY)

    def tiles(*lead):
        return pltpu.VMEM(lead + (8, DEPTH), jnp.float32)

    return pl.pallas_call(
        kernel,
        out_shape=jax.ShapeDtypeStruct((16, 5, BS, BS, DEPTH), jnp.float32),
        in_specs=[smem, smem, hbm, hbm, hbm, vmem, vmem],
        out_specs=hbm,
        scratch_shapes=[
            pltpu.VMEM((5, XE, SIDE, DEPTH), jnp.float32),
            tiles(5, XE),
            tiles(5, XE, TILES + 1),
            pltpu.VMEM((5, SIDE, SIDE, DEPTH), jnp.float32),
            pltpu.VMEM((5, BS, BS, DEPTH), jnp.float32),
            tiles(5, TILES + 1),
            tiles(5, TILES + 1),
            tiles(5, 4, TILES),
            tiles(5, 4, TILES),
            tiles(2, 5, XE),
            tiles(NB, 3),
            pltpu.VMEM((2, SIDE, DEPTH), jnp.float32),
            pltpu.SemaphoreType.DMA((SIDE // CHUNK,)),
            pltpu.SemaphoreType.DMA((4,)),
            pltpu.SemaphoreType.DMA((16,)),
            pltpu.SemaphoreType.DMA((4,)),
        ],
        compiler_params=pltpu.CompilerParams(vmem_limit_bytes=51 * 1024 * 1024),
        cost_estimate=pl.CostEstimate(flops=50_000_000, bytes_accessed=14_000_000, transcendentals=600_000),
    )(level, owner, cons, xlo, xhi, ylo, yhi)


def shifted(block, axis, step):
    n = lax.axis_size(axis)
    return lax.ppermute(block, axis, [(i, (i + step) % n) for i in range(n)])


def x_pack(cells, levels):
    plane = jnp.broadcast_to(jnp.repeat(levels, BS)[None, None, :, None], (1, 2, SIDE, DEPTH))
    return jnp.concatenate([cells, plane], axis=0)


def y_pack(cons, xlo, xhi, levels, at):
    cells = jnp.concatenate([xlo[:5, :, at], cons[:, :, at], xhi[:5, :, at]], axis=1)
    plane = jnp.pad(jnp.repeat(levels, BS), (2, 2))
    plane = jnp.broadcast_to(plane[None, :, None, None], (1, XE, 2, DEPTH))
    return jnp.concatenate([cells, plane], axis=0)


def body(conserved, box_level, box_owner):
    rows = ("gy", "cores")
    lev = box_level.astype(jnp.float32)
    xlo = shifted(x_pack(conserved[:, SIDE - 2 :], lev[NB - 1]), "gx", 1)
    xhi = shifted(x_pack(conserved[:, :2], lev[0]), "gx", -1)
    ylo = shifted(y_pack(conserved, xlo, xhi, lev[:, NB - 1], slice(SIDE - 2, SIDE)), rows, 1)
    yhi = shifted(y_pack(conserved, xlo, xhi, lev[:, 0], slice(0, 2)), rows, -1)
    send = update(box_level.reshape(-1), box_owner.reshape(-1), conserved, xlo, xhi, ylo, yhi)
    return lax.all_to_all(send, "gx", split_axis=0, concat_axis=0, tiled=True)


def solution(mesh):
    rows = ("gy", "cores")
    return jax.shard_map(
        body,
        mesh=mesh,
        in_specs=(P(None, "gx", rows, None), P("gx", rows), P("gx", rows)),
        out_specs=P(("gx", "gy", "cores"), None, None, None, None),
        check_vma=False,
    )
```

```python
import functools

import jax
import jax.numpy as jnp
from jax import lax
from jax.experimental import pallas as pl
from jax.experimental.pallas import tpu as pltpu
from jax.sharding import PartitionSpec as P

BS = 16
NB = 2
SIDE = BS * NB
DEPTH = 128
XE = SIDE + 4
GAMMA = 1.4
STEP = 0.06
HALF = 0.25 * STEP

TILES = 4
HALO = 4
CHUNK = 8

QX = BS // 4
PACKET = (5, QX, BS, DEPTH)
OWN = (21, QX, BS, DEPTH)


def prims(u):
    r, mx, my, mz, e = u
    inv = pl.reciprocal(r, approx=True)
    inv = inv * (2.0 - r * inv)
    vx, vy, vz = mx * inv, my * inv, mz * inv
    p = (GAMMA - 1.0) * (e - 0.5 * (mx * vx + my * vy + mz * vz))
    a = GAMMA * p * inv
    c = a * lax.rsqrt(a)
    return vx, vy, vz, p, c, e + p


def x_side(u, q):
    vx, _, _, p, c, h = q
    return u, [u[1], u[1] * vx + p, u[2] * vx, u[3] * vx, h * vx], jnp.abs(vx) + c


def y_side(u, q):
    _, vy, _, p, c, h = q
    return u, [u[2], u[1] * vy, u[2] * vy + p, u[3] * vy, h * vy], jnp.abs(vy) + c


def z_side(u, q):
    _, _, vz, p, c, h = q
    return u, [u[3], u[1] * vz, u[2] * vz, u[3] * vz + p, h * vz], jnp.abs(vz) + c


def rusanov(lower, upper):
    ua, fa, sa = lower
    ub, fb, sb = upper
    s = jnp.maximum(sa, sb)
    return [(fa[c] + fb[c]) - s * (ub[c] - ua[c]) for c in range(5)]


def each(side, f, shared):
    u, fl, s = side
    nu = [f(v) for v in u]
    return nu, [nu[shared]] + [f(v) for v in fl[1:]], f(s)


def both(pred, a, b, shared):
    ua, fa, sa = a
    ub, fb, sb = b
    u = [jnp.where(pred, v, w) for v, w in zip(ua, ub)]
    f = [u[shared]] + [jnp.where(pred, v, w) for v, w in zip(fa[1:], fb[1:])]
    return u, f, jnp.where(pred, sa, sb)


def z_faces(side, first, last):
    u, fz, sz = side
    face = rusanov(side, each(side, lambda v: pltpu.roll(v, DEPTH - 1, 1), 3))
    wall = 2.0 * fz[3]
    push = 2.0 * sz * u[3]
    walls = jnp.where(first, wall - push, jnp.where(last, -wall - push, 0.0))
    return [jnp.where(last, 0.0, f) for f in face], walls


def kernel(
    level, owner, cons, xlo, xhi, ylo_in, yhi_in, own0, own1, own2, own3,
    wn, wg, md, out, note, fxp, fzp, fxw, fxm, fyw, msk, lvx, ylo, yhi, in_sem, x_sem, y_sem, out_sem, note_sem,
):
    def part(x):
        return pltpu.make_async_copy(
            cons.at[:, pl.ds(x - 2, CHUNK)], wn.at[:, pl.ds(x, CHUNK)], in_sem.at[(x - 2) // CHUNK]
        )

    low = pltpu.make_async_copy(xlo.at[pl.ds(0, 5)], wn.at[:, pl.ds(0, 2)], x_sem.at[0])
    high = pltpu.make_async_copy(xhi.at[pl.ds(0, 5)], wn.at[:, pl.ds(SIDE + 2, 2)], x_sem.at[1])
    low_level = pltpu.make_async_copy(xlo.at[5, 0], lvx.at[0], x_sem.at[2])
    high_level = pltpu.make_async_copy(xhi.at[5, 0], lvx.at[1], x_sem.at[3])
    y_copies = [pltpu.make_async_copy(ylo_in, ylo, y_sem.at[0]), pltpu.make_async_copy(yhi_in, yhi, y_sem.at[1])]
    for copy in y_copies:
        copy.start()
    low.start()
    for i in range(SIDE // CHUNK):
        part(2 + CHUNK * i).start()
    for copy in (high, low_level, high_level):
        copy.start()

    lev = [[level[NB * a + b].astype(jnp.float32) for b in range(NB)] for a in range(NB)]

    for copy in y_copies:
        copy.wait()

    def stage(x, _):
        for c in range(5):
            wg[c, x, 0:1, :] = ylo[c, x, 1:2, :]
            wg[c, x, 1:2, :] = ylo[c, x, 0:1, :]
            wg[c, x, 6:7, :] = yhi[c, x, 1:2, :]
            wg[c, x, 7:8, :] = yhi[c, x, 0:1, :]
        return 0

    lax.fori_loop(0, XE, stage, 0, unroll=2)

    lane = lax.broadcasted_iota(jnp.int32, (8, DEPTH), 1)
    sub = lax.broadcasted_iota(jnp.int32, (8, DEPTH), 0)
    first, last = lane == 0, lane == DEPTH - 1
    bottom, top = sub == 0, sub == 7

    for a in range(NB):
        coarse = [1.0 - lev[a][b] for b in range(NB)]
        below = ylo[5, 2 + BS * a, 0:1, :]
        above = yhi[5, 2 + BS * a, 0:1, :]
        msk[a, 0, :, :] = jnp.where(sub < 4, lev[a][0], lev[a][1])
        msk[a, 1, :, :] = jnp.where(
            sub == 3, HALF * coarse[0] * lev[a][1], jnp.where(top, HALF * coarse[1] * above, 0.0)
        )
        msk[a, 2, :, :] = jnp.where(
            sub == 4, HALF * coarse[1] * lev[a][0], jnp.where(bottom, HALF * coarse[0] * below, 0.0)
        )

    def spread(ref, c, x, t):
        return ref[c, x, pl.ds(t, 8, stride=4), :]

    def load_w(x, t):
        if t == HALO:
            return [wg[c, x] for c in range(5)]
        return [spread(wn, c, x, t) for c in range(5)]

    def load_m(x, t):
        return [md[c, x, t] for c in range(5)]

    def keep_x(t, side):
        _, f, s = side
        for c in range(4):
            fxp[c, t] = f[c + 1]
        fxp[4, t] = s

    def x_face(load, x, t, side):
        u = load(x - 1, t)
        return rusanov((u, [u[1]] + [fxp[c, t] for c in range(4)], fxp[4, t]), side)

    def up(v):
        return pltpu.roll(v, 7, 0)

    def down(v):
        return pltpu.roll(v, 1, 0)

    def z_change(t):
        f = [fzp[c, t] for c in range(5)]
        return [v - pltpu.roll(v, 1, 1) for v in f]

    def sweep(load, x, whole):
        cells, faces, ends, change, side = [], [], [], [], []
        for t in range(TILES + 1):
            u = load(x, t)
            q = prims(u)
            side.append(y_side(u, q))
            if t < TILES or whole:
                sx = x_side(u, q)
                face = x_face(load, x, t, sx)
                keep_x(t, sx)
                dz = z_change(t)
                fz, walls = z_faces(z_side(u, q), first, last)
                for c in range(5):
                    fzp[c, t] = fz[c]
                cells.append(u)
                faces.append(face)
                ends.append([face[c] + dz[c] for c in range(5)])
                change.append([face[c] + walls if c == 3 else face[c] for c in range(5)])
            if 0 < t < TILES:
                fy = rusanov(side[t - 1], side[t])
                change[t - 1] = [change[t - 1][c] - fy[c] for c in range(5)]
                change[t] = [change[t][c] + fy[c] for c in range(5)]
        inner = rusanov(side[3], each(side[0], up, 2))
        edge = rusanov(both(top, side[3], side[4], 2), both(top, side[4], side[0], 2))
        after = [jnp.where(top, edge[c], inner[c]) for c in range(5)]
        before = [jnp.where(bottom, edge[c], down(inner[c])) for c in range(5)]
        change[3] = [change[3][c] - after[c] for c in range(5)]
        change[0] = [change[0][c] + before[c] for c in range(5)]
        if whole:
            outer = rusanov(both(top, side[4], each(side[4], up, 2), 2), both(top, each(side[4], down, 2), side[4], 2))
            for c in range(5):
                d = edge[c] - outer[c]
                change[4][c] = change[4][c] + jnp.where(top, d, -d)
        return cells, faces, ends, change, before, after

    def face_slot(x):
        back = x - 2
        return jnp.where(back % BS == 0, back // BS, 3)

    low.wait()
    for t in range(TILES + 1):
        u = load_w(0, t)
        keep_x(t, x_side(u, prims(u)))

    def first_step(x, _):
        @pl.when(((x - 2) % CHUNK == 0) & (x < SIDE + 2))
        def _():
            part(x).wait()

        @pl.when(x == SIDE + 2)
        def _():
            high.wait()

        slot = face_slot(x)
        cells, faces, ends, change, before, after = sweep(load_w, x, True)
        for c in range(5):
            for t in range(TILES + 1):
                md[c, x - 1, t] = md[c, x - 1, t] - HALF * ends[t][c]
                md[c, x, t] = cells[t][c] + HALF * change[t][c]
                if t < TILES:
                    fxw[c, slot, t] = faces[t][c]
            fyw[0, c, x] = before[c]
            fyw[1, c, x] = after[c]
        return 0

    lax.fori_loop(1, XE, first_step, 0)

    for t in range(TILES):
        u = load_m(1, t)
        keep_x(t, x_side(u, prims(u)))

    def second_step(x, _):
        slot = face_slot(x)
        row = jnp.maximum(x - 3, 0)
        fine_back = HALF * msk[row // BS, 0]
        a = (x - 2) // BS
        fine = msk[a, 0]
        coarse = 1.0 - fine
        fine_here = HALF * fine
        at_top, at_bottom = msk[a, 1], msk[a, 2]
        cells, faces, ends, change, before, after = sweep(load_m, x, False)
        for c in range(5):
            for t in range(TILES):
                fxm[c, slot, t] = faces[t][c]
                at = pl.ds(t, 8, stride=4)
                out[c, row, at, :] = out[c, row, at, :] - fine_back * ends[t][c]
                u = cells[t][c]
                v = u + coarse * (u - spread(wn, c, x, t)) + fine_here * change[t][c]
                if t == 0:
                    v = v + at_bottom * (before[c] - fyw[0, c, x])
                if t == 3:
                    v = v - at_top * (after[c] - fyw[1, c, x])
                out[c, x - 2, at, :] = v
        return 0

    def correct(k):
        below = lvx[0, pl.ds(0, 8, stride=4), :] if k == 0 else msk[k - 1, 0]
        above = lvx[1, pl.ds(0, 8, stride=4), :] if k == NB else msk[k, 0]
        to_below = (HALF * (1.0 - below)) * above
        to_above = (HALF * (1.0 - above)) * below
        for t in range(TILES):
            at = pl.ds(t, 8, stride=4)
            for c in range(5):
                d = fxm[c, k, t] - fxw[c, k, t]
                if k > 0:
                    out[c, BS * k - 1, at, :] = out[c, BS * k - 1, at, :] - to_below * d
                if k < NB:
                    out[c, BS * k, at, :] = out[c, BS * k, at, :] + to_above * d

    done = []
    for i in range(NB * NB):
        note[i] = jnp.full((BS, DEPTH), corner(owner[i]).astype(jnp.float32))
    for q, own in enumerate((own0, own1, own2, own3)):
        copy = pltpu.make_async_copy(note, own.at[20], note_sem.at[q])
        copy.start()
        done.append(copy)

    def ship(a):
        for b in range(NB):
            for q, own in enumerate((own0, own1, own2, own3)):
                i = NB * a + b
                copy = pltpu.make_async_copy(
                    out.at[:, pl.ds(BS * a + QX * q, QX), pl.ds(BS * b, BS), :], own.at[pl.ds(5 * i, 5)], out_sem.at[i, q]
                )
                copy.start()
                done.append(copy)

    lax.fori_loop(2, BS + 3, second_step, 0)
    low_level.wait()
    high_level.wait()
    correct(0)
    correct(1)
    ship(0)
    lax.fori_loop(BS + 3, SIDE + 2, second_step, 0)
    for t in range(TILES):
        u = load_m(SIDE + 2, t)
        face = x_face(load_m, SIDE + 2, t, x_side(u, prims(u)))
        dz = z_change(t)
        at = pl.ds(t, 8, stride=4)
        for c in range(5):
            fxm[c, 2, t] = face[c]
            out[c, SIDE - 1, at, :] = out[c, SIDE - 1, at, :] - (HALF * msk[NB - 1, 0]) * (face[c] + dz[c])
    correct(2)
    ship(1)
    for copy in done:
        copy.wait()


def update(level, owner, cons, xlo, xhi, ylo, yhi):
    smem = pl.BlockSpec(memory_space=pltpu.SMEM)
    hbm = pl.BlockSpec(memory_space=pl.ANY)

    def tiles(*lead):
        return pltpu.VMEM(lead + (8, DEPTH), jnp.float32)

    return pl.pallas_call(
        kernel,
        out_shape=[jax.ShapeDtypeStruct(OWN, jnp.float32)] * 4,
        in_specs=[smem, smem, hbm, hbm, hbm, hbm, hbm],
        out_specs=[hbm] * 4,
        scratch_shapes=[
            pltpu.VMEM((5, XE, SIDE, DEPTH), jnp.float32),
            tiles(5, XE),
            tiles(5, XE, TILES + 1),
            pltpu.VMEM((5, SIDE, SIDE, DEPTH), jnp.float32),
            pltpu.VMEM((QX, BS, DEPTH), jnp.float32),
            tiles(5, TILES + 1),
            tiles(5, TILES + 1),
            tiles(5, 4, TILES),
            tiles(5, 4, TILES),
            tiles(2, 5, XE),
            tiles(NB, 3),
            pltpu.VMEM((2, SIDE, DEPTH), jnp.float32),
            pltpu.VMEM((6, XE, 2, DEPTH), jnp.float32),
            pltpu.VMEM((6, XE, 2, DEPTH), jnp.float32),
            pltpu.SemaphoreType.DMA((SIDE // CHUNK,)),
            pltpu.SemaphoreType.DMA((4,)),
            pltpu.SemaphoreType.DMA((2,)),
            pltpu.SemaphoreType.DMA((4, 4)),
            pltpu.SemaphoreType.DMA((4,)),
        ],
        compiler_params=pltpu.CompilerParams(vmem_limit_bytes=60 * 1024 * 1024),
        cost_estimate=pl.CostEstimate(flops=50_000_000, bytes_accessed=14_000_000, transcendentals=600_000),
    )(level, owner, cons, xlo, xhi, ylo, yhi)


def corner(g):
    return g ^ ((g >> 1) & 5)


def bit(q, t):
    return 1 << ((q + t) % 4)


def across(block, q, t):
    return lax.ppermute(block, "gx", [(g, corner(corner(g) ^ bit(q, t))) for g in range(16)])


def place(out, me, mask, q):
    return out.at[corner(me ^ mask), :, pl.ds(QX * q, QX)]


def gather(src, me, patterns, stores):
    notes = [src[20, i, 0:8, :] for i in range(4)]
    picks = [[note == (me ^ pattern).astype(jnp.float32) for note in notes] for pattern in patterns]

    def body(c, _):
        for x in range(QX):
            for part in (slice(0, 8), slice(8, 16)):
                cells = [src[5 * i + c, x, part, :] for i in range(4)]
                for pick, store in zip(picks, stores):
                    v = jnp.zeros((8, DEPTH), jnp.float32)
                    for i in range(4):
                        v = jnp.where(pick[i], cells[i], v)
                    store[c, x, part, :] = v
        return 0

    lax.fori_loop(0, 5, body, 0)


def two_kernel(meta, *refs):
    low, high, m2 = refs[0:4], refs[4:8], refs[8:12]
    me = meta[0]
    for q in range(4):
        for f0, src in enumerate((low[q], high[q])):
            patterns = [bit(q, 2) | (b3 * bit(q, 3)) for b3 in range(2)]
            gather(src, me, patterns, [m2[q].at[2 * f0 + b3] for b3 in range(2)])


def four_kernel(meta, *refs):
    arrays, m3 = refs[0:16], refs[16:20]
    for q in range(4):
        for f in range(4):
            gather(arrays[4 * f + q], meta[0], [bit(q, 3)], [m3[q].at[f]])


def end_kernel(meta, *refs):
    arrays, out, buf, sem = refs[0:16], refs[16], refs[17], refs[18]
    me = meta[0]
    copies = []
    for q in range(4):
        for f in range(4):
            f1, f0 = f // 2, f % 2
            gather(arrays[4 * f + q], me, [0], [buf.at[4 * q + f]])
            to = place(out, me, f0 * bit(q, 0) | f1 * bit(q, 1), q)
            copies.append(pltpu.make_async_copy(buf.at[4 * q + f], to, sem.at[4 * q + f]))
            copies[-1].start()
    for copy in copies:
        copy.wait()


def pass_kernel(meta, *refs):
    r2a, r2b, m3b = refs[0:4], refs[4:8], refs[8:12]

    def body(c, _):
        for q in range(4):
            for f in range(4):
                m3b[q][f, c] = (r2a, r2b)[f // 2][q][2 * (f % 2) + 1, c]
        return 0

    lax.fori_loop(0, 5, body, 0)


def place_kernel(kind, flows, meta, *refs):
    n = len(refs) - 3
    arrays, out, sem = refs[:n], refs[-2], refs[-1]
    me = meta[0]
    copies = []
    for i, q in enumerate(flows):
        for f in range(4):
            f1, f0 = f // 2, f % 2
            mask = f0 * bit(q, 0) | f1 * bit(q, 1)
            if kind == 2:
                src, mask = arrays[len(flows) * f1 + i].at[2 * f0], mask | bit(q, 2)
            else:
                src, mask = arrays[i].at[f], mask | ((kind - 3) * bit(q, 2)) | bit(q, 3)
            copies.append(pltpu.make_async_copy(src, place(out, me, mask, q), sem.at[4 * i + f]))
    for copy in copies:
        copy.start()
    for copy in copies:
        copy.wait()


MOVED = jax.ShapeDtypeStruct((4,) + PACKET, jnp.float32)
RESULT = jax.ShapeDtypeStruct((16, 5, BS, BS, DEPTH), jnp.float32)


def mover(f, outs, meta, *args):
    hbm = pl.BlockSpec(memory_space=pl.ANY)
    vmem = pl.BlockSpec(memory_space=pltpu.VMEM)
    end = outs[0] is RESULT
    return pl.pallas_call(
        f,
        out_shape=outs,
        in_specs=[pl.BlockSpec(memory_space=pltpu.SMEM)] + [vmem] * len(args),
        out_specs=[hbm if end else vmem] * len(outs),
        scratch_shapes=[pltpu.VMEM((16,) + PACKET, jnp.float32), pltpu.SemaphoreType.DMA((16,))] if end else [],
        compiler_params=pltpu.CompilerParams(vmem_limit_bytes=18 * 1024 * 1024),
        cost_estimate=pl.CostEstimate(flops=0, bytes_accessed=8_000_000, transcendentals=0),
    )(meta, *args)


def placer(kind, flows, meta, arrays, out):
    vmem = pl.BlockSpec(memory_space=pltpu.VMEM)
    hbm = pl.BlockSpec(memory_space=pl.ANY)
    return pl.pallas_call(
        functools.partial(place_kernel, kind, flows),
        out_shape=RESULT,
        in_specs=[pl.BlockSpec(memory_space=pltpu.SMEM)] + [vmem] * len(arrays) + [hbm],
        out_specs=hbm,
        scratch_shapes=[pltpu.SemaphoreType.DMA((4 * len(flows),))],
        input_output_aliases={1 + len(arrays): 0},
        compiler_params=pltpu.CompilerParams(vmem_limit_bytes=8 * 1024 * 1024),
        cost_estimate=pl.CostEstimate(flops=0, bytes_accessed=4_000_000, transcendentals=0),
    )(meta, *arrays, out)


def relocate(own):
    meta = corner(lax.axis_index("gx")).astype(jnp.int32)[None]
    flows = range(4)
    r0 = [across(own[q], q, 0) for q in flows]
    r1a = [across(own[q], q, 1) for q in flows]
    r1b = [across(r0[q], q, 1) for q in flows]
    m2a = mover(two_kernel, [MOVED] * 4, meta, *own, *r0)
    r2a = [across(m2a[q], q, 2) for q in flows]
    m2b = mover(two_kernel, [MOVED] * 4, meta, *r1a, *r1b)
    r2b = [across(m2b[q], q, 2) for q in flows]
    m3a = mover(four_kernel, [MOVED] * 4, meta, *own, *r0, *r1a, *r1b)
    r3a = [across(m3a[q], q, 3) for q in flows]
    m3b = mover(pass_kernel, [MOVED] * 4, meta, *r2a, *r2b)
    r3b = [across(m3b[q], q, 3) for q in flows]
    (out,) = mover(end_kernel, [RESULT], meta, *own, *r0, *r1a, *r1b)
    out = placer(2, (0, 1, 2, 3), meta, r2a + r2b, out)
    out = placer(3, (0, 1, 2, 3), meta, r3a, out)
    out = placer(4, (0, 1), meta, r3b[:2], out)
    return placer(4, (2, 3), meta, r3b[2:], out)


def shifted(block, axis, step):
    n = lax.axis_size(axis)
    return lax.ppermute(block, axis, [(i, (i + step) % n) for i in range(n)])


def x_pack(cells, levels):
    plane = jnp.broadcast_to(jnp.repeat(levels, BS)[None, None, :, None], (1, 2, SIDE, DEPTH))
    return jnp.concatenate([cells, plane], axis=0)


def y_pack(cons, xlo, xhi, levels, at):
    cells = jnp.concatenate([xlo[:5, :, at], cons[:, :, at], xhi[:5, :, at]], axis=1)
    plane = jnp.pad(jnp.repeat(levels, BS), (2, 2))
    plane = jnp.broadcast_to(plane[None, :, None, None], (1, XE, 2, DEPTH))
    return jnp.concatenate([cells, plane], axis=0)


def body(conserved, box_level, box_owner):
    rows = ("gy", "cores")
    lev = box_level.astype(jnp.float32)
    xlo = shifted(x_pack(conserved[:, SIDE - 2 :], lev[NB - 1]), "gx", 1)
    xhi = shifted(x_pack(conserved[:, :2], lev[0]), "gx", -1)
    ylo = shifted(y_pack(conserved, xlo, xhi, lev[:, NB - 1], slice(SIDE - 2, SIDE)), rows, 1)
    yhi = shifted(y_pack(conserved, xlo, xhi, lev[:, 0], slice(0, 2)), rows, -1)
    owner = box_owner.reshape(-1)
    own = update(box_level.reshape(-1), owner, conserved, xlo, xhi, ylo, yhi)
    return relocate(own)


def solution(mesh):
    rows = ("gy", "cores")
    return jax.shard_map(
        body,
        mesh=mesh,
        in_specs=(P(None, "gx", rows, None), P("gx", rows), P("gx", rows)),
        out_specs=P(("gx", "gy", "cores"), None, None, None, None),
        check_vma=False,
    )
```

```python
import functools

import jax
import jax.numpy as jnp
from jax import lax
from jax.experimental import pallas as pl
from jax.experimental.pallas import tpu as pltpu
from jax.sharding import PartitionSpec as P

BS = 16
NB = 2
SIDE = BS * NB
DEPTH = 128
XE = SIDE + 4
GAMMA = 1.4
STEP = 0.06
HALF = 0.25 * STEP

TILES = 4
HALO = 4
CHUNK = 8

QX = BS // 4
PACKET = (5, QX, BS, DEPTH)
OWN = (21, QX, BS, DEPTH)


def prims(u):
    r, mx, my, mz, e = u
    inv = pl.reciprocal(r, approx=True)
    inv = inv * (2.0 - r * inv)
    vx, vy, vz = mx * inv, my * inv, mz * inv
    p = (GAMMA - 1.0) * (e - 0.5 * (mx * vx + my * vy + mz * vz))
    a = GAMMA * p * inv
    c = a * lax.rsqrt(a)
    return vx, vy, vz, p, c, e + p


def x_side(u, q):
    vx, _, _, p, c, h = q
    return u, [u[1], u[1] * vx + p, u[2] * vx, u[3] * vx, h * vx], jnp.abs(vx) + c


def y_side(u, q):
    _, vy, _, p, c, h = q
    return u, [u[2], u[1] * vy, u[2] * vy + p, u[3] * vy, h * vy], jnp.abs(vy) + c


def z_side(u, q):
    _, _, vz, p, c, h = q
    return u, [u[3], u[1] * vz, u[2] * vz, u[3] * vz + p, h * vz], jnp.abs(vz) + c


def rusanov(lower, upper):
    ua, fa, sa = lower
    ub, fb, sb = upper
    s = jnp.maximum(sa, sb)
    return [(fa[c] + fb[c]) - s * (ub[c] - ua[c]) for c in range(5)]


def each(side, f, shared):
    u, fl, s = side
    nu = [f(v) for v in u]
    return nu, [nu[shared]] + [f(v) for v in fl[1:]], f(s)


def both(pred, a, b, shared):
    ua, fa, sa = a
    ub, fb, sb = b
    u = [jnp.where(pred, v, w) for v, w in zip(ua, ub)]
    f = [u[shared]] + [jnp.where(pred, v, w) for v, w in zip(fa[1:], fb[1:])]
    return u, f, jnp.where(pred, sa, sb)


def z_faces(side, first, last):
    u, fz, sz = side
    face = rusanov(side, each(side, lambda v: pltpu.roll(v, DEPTH - 1, 1), 3))
    wall = 2.0 * fz[3]
    push = 2.0 * sz * u[3]
    walls = jnp.where(first, wall - push, jnp.where(last, -wall - push, 0.0))
    return [jnp.where(last, 0.0, f) for f in face], walls


def kernel(
    level, owner, cons, xlo, xhi, ylo_in, yhi_in, own0, own1, own2, own3,
    wn, wg, md, out, note, fxp, fzp, fxw, fxm, fyw, msk, lvx, ylo, yhi, in_sem, x_sem, y_sem, out_sem, note_sem,
):
    def part(x):
        return pltpu.make_async_copy(
            cons.at[:, pl.ds(x - 2, CHUNK)], wn.at[:, pl.ds(x, CHUNK)], in_sem.at[(x - 2) // CHUNK]
        )

    low = pltpu.make_async_copy(xlo.at[pl.ds(0, 5)], wn.at[:, pl.ds(0, 2)], x_sem.at[0])
    high = pltpu.make_async_copy(xhi.at[pl.ds(0, 5)], wn.at[:, pl.ds(SIDE + 2, 2)], x_sem.at[1])
    low_level = pltpu.make_async_copy(xlo.at[5, 0], lvx.at[0], x_sem.at[2])
    high_level = pltpu.make_async_copy(xhi.at[5, 0], lvx.at[1], x_sem.at[3])
    y_copies = [pltpu.make_async_copy(ylo_in, ylo, y_sem.at[0]), pltpu.make_async_copy(yhi_in, yhi, y_sem.at[1])]
    for copy in y_copies:
        copy.start()
    low.start()
    for i in range(SIDE // CHUNK):
        part(2 + CHUNK * i).start()
    for copy in (high, low_level, high_level):
        copy.start()

    lev = [[level[NB * a + b].astype(jnp.float32) for b in range(NB)] for a in range(NB)]

    for copy in y_copies:
        copy.wait()

    def stage(x, _):
        for c in range(5):
            wg[c, x, 0:1, :] = ylo[c, x, 1:2, :]
            wg[c, x, 1:2, :] = ylo[c, x, 0:1, :]
            wg[c, x, 6:7, :] = yhi[c, x, 1:2, :]
            wg[c, x, 7:8, :] = yhi[c, x, 0:1, :]
        return 0

    lax.fori_loop(0, XE, stage, 0, unroll=2)

    lane = lax.broadcasted_iota(jnp.int32, (8, DEPTH), 1)
    sub = lax.broadcasted_iota(jnp.int32, (8, DEPTH), 0)
    first, last = lane == 0, lane == DEPTH - 1
    bottom, top = sub == 0, sub == 7

    for a in range(NB):
        coarse = [1.0 - lev[a][b] for b in range(NB)]
        below = ylo[5, 2 + BS * a, 0:1, :]
        above = yhi[5, 2 + BS * a, 0:1, :]
        msk[a, 0, :, :] = jnp.where(sub < 4, lev[a][0], lev[a][1])
        msk[a, 1, :, :] = jnp.where(
            sub == 3, HALF * coarse[0] * lev[a][1], jnp.where(top, HALF * coarse[1] * above, 0.0)
        )
        msk[a, 2, :, :] = jnp.where(
            sub == 4, HALF * coarse[1] * lev[a][0], jnp.where(bottom, HALF * coarse[0] * below, 0.0)
        )

    def spread(ref, c, x, t):
        return ref[c, x, pl.ds(t, 8, stride=4), :]

    def load_w(x, t):
        if t == HALO:
            return [wg[c, x] for c in range(5)]
        return [spread(wn, c, x, t) for c in range(5)]

    def load_m(x, t):
        return [md[c, x, t] for c in range(5)]

    def keep_x(t, side):
        _, f, s = side
        for c in range(4):
            fxp[c, t] = f[c + 1]
        fxp[4, t] = s

    def x_face(load, x, t, side):
        u = load(x - 1, t)
        return rusanov((u, [u[1]] + [fxp[c, t] for c in range(4)], fxp[4, t]), side)

    def up(v):
        return pltpu.roll(v, 7, 0)

    def down(v):
        return pltpu.roll(v, 1, 0)

    def z_change(t):
        f = [fzp[c, t] for c in range(5)]
        return [v - pltpu.roll(v, 1, 1) for v in f]

    def sweep(load, x, whole, end_row):
        cells, change, side = [], [], []
        for t in range(TILES + 1):
            u = load(x, t)
            q = prims(u)
            side.append(y_side(u, q))
            if t < TILES or whole:
                sx = x_side(u, q)
                face = x_face(load, x, t, sx)
                keep_x(t, sx)
                dz = z_change(t)
                fz, walls = z_faces(z_side(u, q), first, last)
                for c in range(5):
                    fzp[c, t] = fz[c]
                cells.append(u)
                end_row(t, face, dz)
                change.append([face[c] + walls if c == 3 else face[c] for c in range(5)])
            if 0 < t < TILES:
                fy = rusanov(side[t - 1], side[t])
                change[t - 1] = [change[t - 1][c] - fy[c] for c in range(5)]
                change[t] = [change[t][c] + fy[c] for c in range(5)]
        inner = rusanov(side[3], each(side[0], up, 2))
        edge = rusanov(both(top, side[3], side[4], 2), both(top, side[4], side[0], 2))
        after = [jnp.where(top, edge[c], inner[c]) for c in range(5)]
        before = [jnp.where(bottom, edge[c], down(inner[c])) for c in range(5)]
        change[3] = [change[3][c] - after[c] for c in range(5)]
        change[0] = [change[0][c] + before[c] for c in range(5)]
        if whole:
            outer = rusanov(both(top, side[4], each(side[4], up, 2), 2), both(top, each(side[4], down, 2), side[4], 2))
            for c in range(5):
                d = edge[c] - outer[c]
                change[4][c] = change[4][c] + jnp.where(top, d, -d)
        return cells, change, before, after

    def face_slot(x):
        back = x - 2
        return jnp.where(back % BS == 0, back // BS, 3)

    low.wait()
    for t in range(TILES + 1):
        u = load_w(0, t)
        keep_x(t, x_side(u, prims(u)))

    def first_step(x, _):
        @pl.when(((x - 2) % CHUNK == 0) & (x < SIDE + 2))
        def _():
            part(x).wait()

        @pl.when(x == SIDE + 2)
        def _():
            high.wait()

        slot = face_slot(x)

        def end_row(t, face, dz):
            for c in range(5):
                md[c, x - 1, t] = md[c, x - 1, t] - HALF * (face[c] + dz[c])
                if t < TILES:
                    fxw[c, slot, t] = face[c]

        cells, change, before, after = sweep(load_w, x, True, end_row)
        for c in range(5):
            for t in range(TILES + 1):
                md[c, x, t] = cells[t][c] + HALF * change[t][c]
            fyw[0, c, x] = before[c]
            fyw[1, c, x] = after[c]
        return 0

    lax.fori_loop(1, XE, first_step, 0)

    for t in range(TILES):
        u = load_m(1, t)
        keep_x(t, x_side(u, prims(u)))

    def second_step(x, _):
        slot = face_slot(x)
        row = jnp.maximum(x - 3, 0)
        fine_back = HALF * msk[row // BS, 0]
        a = (x - 2) // BS
        fine = msk[a, 0]
        coarse = 1.0 - fine
        fine_here = HALF * fine
        at_top, at_bottom = msk[a, 1], msk[a, 2]

        def end_row(t, face, dz):
            at = pl.ds(t, 8, stride=4)
            for c in range(5):
                fxm[c, slot, t] = face[c]
                out[c, row, at, :] = out[c, row, at, :] - fine_back * (face[c] + dz[c])

        cells, change, before, after = sweep(load_m, x, False, end_row)
        for c in range(5):
            for t in range(TILES):
                at = pl.ds(t, 8, stride=4)
                u = cells[t][c]
                v = u + coarse * (u - spread(wn, c, x, t)) + fine_here * change[t][c]
                if t == 0:
                    v = v + at_bottom * (before[c] - fyw[0, c, x])
                if t == 3:
                    v = v - at_top * (after[c] - fyw[1, c, x])
                out[c, x - 2, at, :] = v
        return 0

    def correct(k):
        below = lvx[0, pl.ds(0, 8, stride=4), :] if k == 0 else msk[k - 1, 0]
        above = lvx[1, pl.ds(0, 8, stride=4), :] if k == NB else msk[k, 0]
        to_below = (HALF * (1.0 - below)) * above
        to_above = (HALF * (1.0 - above)) * below
        for t in range(TILES):
            at = pl.ds(t, 8, stride=4)
            for c in range(5):
                d = fxm[c, k, t] - fxw[c, k, t]
                if k > 0:
                    out[c, BS * k - 1, at, :] = out[c, BS * k - 1, at, :] - to_below * d
                if k < NB:
                    out[c, BS * k, at, :] = out[c, BS * k, at, :] + to_above * d

    done = []
    for i in range(NB * NB):
        note[i] = jnp.full((BS, DEPTH), corner(owner[i]).astype(jnp.float32))
    for q, own in enumerate((own0, own1, own2, own3)):
        copy = pltpu.make_async_copy(note, own.at[20], note_sem.at[q])
        copy.start()
        done.append(copy)

    def ship(a):
        for b in range(NB):
            for q, own in enumerate((own0, own1, own2, own3)):
                i = NB * a + b
                copy = pltpu.make_async_copy(
                    out.at[:, pl.ds(BS * a + QX * q, QX), pl.ds(BS * b, BS), :], own.at[pl.ds(5 * i, 5)], out_sem.at[i, q]
                )
                copy.start()
                done.append(copy)

    lax.fori_loop(2, BS + 3, second_step, 0)
    low_level.wait()
    high_level.wait()
    correct(0)
    correct(1)
    ship(0)
    lax.fori_loop(BS + 3, SIDE + 2, second_step, 0)
    for t in range(TILES):
        u = load_m(SIDE + 2, t)
        face = x_face(load_m, SIDE + 2, t, x_side(u, prims(u)))
        dz = z_change(t)
        at = pl.ds(t, 8, stride=4)
        for c in range(5):
            fxm[c, 2, t] = face[c]
            out[c, SIDE - 1, at, :] = out[c, SIDE - 1, at, :] - (HALF * msk[NB - 1, 0]) * (face[c] + dz[c])
    correct(2)
    ship(1)
    for copy in done:
        copy.wait()


def update(level, owner, cons, xlo, xhi, ylo, yhi):
    smem = pl.BlockSpec(memory_space=pltpu.SMEM)
    hbm = pl.BlockSpec(memory_space=pl.ANY)

    def tiles(*lead):
        return pltpu.VMEM(lead + (8, DEPTH), jnp.float32)

    return pl.pallas_call(
        kernel,
        out_shape=[jax.ShapeDtypeStruct(OWN, jnp.float32)] * 4,
        in_specs=[smem, smem, hbm, hbm, hbm, hbm, hbm],
        out_specs=[hbm] * 4,
        scratch_shapes=[
            pltpu.VMEM((5, XE, SIDE, DEPTH), jnp.float32),
            tiles(5, XE),
            tiles(5, XE, TILES + 1),
            pltpu.VMEM((5, SIDE, SIDE, DEPTH), jnp.float32),
            pltpu.VMEM((QX, BS, DEPTH), jnp.float32),
            tiles(5, TILES + 1),
            tiles(5, TILES + 1),
            tiles(5, 4, TILES),
            tiles(5, 4, TILES),
            tiles(2, 5, XE),
            tiles(NB, 3),
            pltpu.VMEM((2, SIDE, DEPTH), jnp.float32),
            pltpu.VMEM((6, XE, 2, DEPTH), jnp.float32),
            pltpu.VMEM((6, XE, 2, DEPTH), jnp.float32),
            pltpu.SemaphoreType.DMA((SIDE // CHUNK,)),
            pltpu.SemaphoreType.DMA((4,)),
            pltpu.SemaphoreType.DMA((2,)),
            pltpu.SemaphoreType.DMA((4, 4)),
            pltpu.SemaphoreType.DMA((4,)),
        ],
        compiler_params=pltpu.CompilerParams(vmem_limit_bytes=60 * 1024 * 1024),
        cost_estimate=pl.CostEstimate(flops=50_000_000, bytes_accessed=14_000_000, transcendentals=600_000),
    )(level, owner, cons, xlo, xhi, ylo, yhi)


def corner(g):
    return g ^ ((g >> 1) & 5)


def bit(q, t):
    return 1 << ((q + t) % 4)


def across(block, q, t):
    return lax.ppermute(block, "gx", [(g, corner(corner(g) ^ bit(q, t))) for g in range(16)])


def place(out, me, mask, q):
    return out.at[corner(me ^ mask), :, pl.ds(QX * q, QX)]


def gather(src, me, patterns, stores):
    notes = [src[20, i, 0:8, :] for i in range(4)]
    picks = [[note == (me ^ pattern).astype(jnp.float32) for note in notes] for pattern in patterns]

    def body(c, _):
        for x in range(QX):
            for part in (slice(0, 8), slice(8, 16)):
                cells = [src[5 * i + c, x, part, :] for i in range(4)]
                for pick, store in zip(picks, stores):
                    v = jnp.zeros((8, DEPTH), jnp.float32)
                    for i in range(4):
                        v = jnp.where(pick[i], cells[i], v)
                    store[c, x, part, :] = v
        return 0

    lax.fori_loop(0, 5, body, 0)


def two_kernel(meta, *refs):
    low, high, m2 = refs[0:4], refs[4:8], refs[8:12]
    me = meta[0]
    for q in range(4):
        for f0, src in enumerate((low[q], high[q])):
            patterns = [bit(q, 2) | (b3 * bit(q, 3)) for b3 in range(2)]
            gather(src, me, patterns, [m2[q].at[2 * f0 + b3] for b3 in range(2)])


def four_kernel(meta, *refs):
    arrays, m3 = refs[0:16], refs[16:20]
    for q in range(4):
        for f in range(4):
            gather(arrays[4 * f + q], meta[0], [bit(q, 3)], [m3[q].at[f]])


def end_kernel(meta, *refs):
    arrays, out, buf, sem = refs[0:16], refs[16], refs[17], refs[18]
    me = meta[0]
    copies = []
    for q in range(4):
        for f in range(4):
            f1, f0 = f // 2, f % 2
            gather(arrays[4 * f + q], me, [0], [buf.at[4 * q + f]])
            to = place(out, me, f0 * bit(q, 0) | f1 * bit(q, 1), q)
            copies.append(pltpu.make_async_copy(buf.at[4 * q + f], to, sem.at[4 * q + f]))
            copies[-1].start()
    for copy in copies:
        copy.wait()


def pass_kernel(meta, *refs):
    r2a, r2b, m3b = refs[0:4], refs[4:8], refs[8:12]

    def body(c, _):
        for q in range(4):
            for f in range(4):
                m3b[q][f, c] = (r2a, r2b)[f // 2][q][2 * (f % 2) + 1, c]
        return 0

    lax.fori_loop(0, 5, body, 0)


def place_kernel(kind, flows, meta, *refs):
    n = len(refs) - 3
    arrays, out, sem = refs[:n], refs[-2], refs[-1]
    me = meta[0]
    copies = []
    for i, q in enumerate(flows):
        for f in range(4):
            f1, f0 = f // 2, f % 2
            mask = f0 * bit(q, 0) | f1 * bit(q, 1)
            if kind == 2:
                src, mask = arrays[len(flows) * f1 + i].at[2 * f0], mask | bit(q, 2)
            else:
                src, mask = arrays[i].at[f], mask | ((kind - 3) * bit(q, 2)) | bit(q, 3)
            copies.append(pltpu.make_async_copy(src, place(out, me, mask, q), sem.at[4 * i + f]))
    for copy in copies:
        copy.start()
    for copy in copies:
        copy.wait()


MOVED = jax.ShapeDtypeStruct((4,) + PACKET, jnp.float32)
RESULT = jax.ShapeDtypeStruct((16, 5, BS, BS, DEPTH), jnp.float32)


def mover(f, outs, meta, *args):
    hbm = pl.BlockSpec(memory_space=pl.ANY)
    vmem = pl.BlockSpec(memory_space=pltpu.VMEM)
    end = outs[0] is RESULT
    return pl.pallas_call(
        f,
        out_shape=outs,
        in_specs=[pl.BlockSpec(memory_space=pltpu.SMEM)] + [vmem] * len(args),
        out_specs=[hbm if end else vmem] * len(outs),
        scratch_shapes=[pltpu.VMEM((16,) + PACKET, jnp.float32), pltpu.SemaphoreType.DMA((16,))] if end else [],
        compiler_params=pltpu.CompilerParams(vmem_limit_bytes=18 * 1024 * 1024),
        cost_estimate=pl.CostEstimate(flops=0, bytes_accessed=8_000_000, transcendentals=0),
    )(meta, *args)


def placer(kind, flows, meta, arrays, out):
    vmem = pl.BlockSpec(memory_space=pltpu.VMEM)
    hbm = pl.BlockSpec(memory_space=pl.ANY)
    return pl.pallas_call(
        functools.partial(place_kernel, kind, flows),
        out_shape=RESULT,
        in_specs=[pl.BlockSpec(memory_space=pltpu.SMEM)] + [vmem] * len(arrays) + [hbm],
        out_specs=hbm,
        scratch_shapes=[pltpu.SemaphoreType.DMA((4 * len(flows),))],
        input_output_aliases={1 + len(arrays): 0},
        compiler_params=pltpu.CompilerParams(vmem_limit_bytes=8 * 1024 * 1024),
        cost_estimate=pl.CostEstimate(flops=0, bytes_accessed=4_000_000, transcendentals=0),
    )(meta, *arrays, out)


def relocate(own):
    meta = corner(lax.axis_index("gx")).astype(jnp.int32)[None]
    flows = range(4)
    r0 = [across(own[q], q, 0) for q in flows]
    r1a = [across(own[q], q, 1) for q in flows]
    r1b = [across(r0[q], q, 1) for q in flows]
    m2a = mover(two_kernel, [MOVED] * 4, meta, *own, *r0)
    r2a = [across(m2a[q], q, 2) for q in flows]
    m2b = mover(two_kernel, [MOVED] * 4, meta, *r1a, *r1b)
    r2b = [across(m2b[q], q, 2) for q in flows]
    m3a = mover(four_kernel, [MOVED] * 4, meta, *own, *r0, *r1a, *r1b)
    r3a = [across(m3a[q], q, 3) for q in flows]
    m3b = mover(pass_kernel, [MOVED] * 4, meta, *r2a, *r2b)
    r3b = [across(m3b[q], q, 3) for q in flows]
    (out,) = mover(end_kernel, [RESULT], meta, *own, *r0, *r1a, *r1b)
    out = placer(2, (0, 1, 2, 3), meta, r2a + r2b, out)
    out = placer(3, (0, 1, 2, 3), meta, r3a, out)
    out = placer(4, (0, 1), meta, r3b[:2], out)
    return placer(4, (2, 3), meta, r3b[2:], out)


def shifted(block, axis, step):
    n = lax.axis_size(axis)
    return lax.ppermute(block, axis, [(i, (i + step) % n) for i in range(n)])


def x_pack(cells, levels):
    plane = jnp.broadcast_to(jnp.repeat(levels, BS)[None, None, :, None], (1, 2, SIDE, DEPTH))
    return jnp.concatenate([cells, plane], axis=0)


def y_pack(cons, xlo, xhi, levels, at):
    cells = jnp.concatenate([xlo[:5, :, at], cons[:, :, at], xhi[:5, :, at]], axis=1)
    plane = jnp.pad(jnp.repeat(levels, BS), (2, 2))
    plane = jnp.broadcast_to(plane[None, :, None, None], (1, XE, 2, DEPTH))
    return jnp.concatenate([cells, plane], axis=0)


def body(conserved, box_level, box_owner):
    rows = ("gy", "cores")
    lev = box_level.astype(jnp.float32)
    xlo = shifted(x_pack(conserved[:, SIDE - 2 :], lev[NB - 1]), "gx", 1)
    xhi = shifted(x_pack(conserved[:, :2], lev[0]), "gx", -1)
    ylo = shifted(y_pack(conserved, xlo, xhi, lev[:, NB - 1], slice(SIDE - 2, SIDE)), rows, 1)
    yhi = shifted(y_pack(conserved, xlo, xhi, lev[:, 0], slice(0, 2)), rows, -1)
    owner = box_owner.reshape(-1)
    own = update(box_level.reshape(-1), owner, conserved, xlo, xhi, ylo, yhi)
    return relocate(own)


def solution(mesh):
    rows = ("gy", "cores")
    return jax.shard_map(
        body,
        mesh=mesh,
        in_specs=(P(None, "gx", rows, None), P("gx", rows), P("gx", rows)),
        out_specs=P(("gx", "gy", "cores"), None, None, None, None),
        check_vma=False,
    )
```
